32 devices in a mesh: parts: 1, seq: 32 (over z, y, x, core).
Axes of the slice: x: 2, y: 2, z: 4, core: 2. Of those that a mesh axis runs over, the one named last changes fastest.
Arguments:
- tokens: bfloat16 [1, 128, 3, 128, 3072], P('parts', 'seq'), may hold values from -6 to 6
- queries: bfloat16 [1, 128, 3, 128, 1536], P('parts', 'seq'), may hold values from -68 to 68
- key_weight: bfloat16 [3072, 1536], P('seq'), may hold values from -0.109375 to 0.109375
- value_weight: bfloat16 [3072, 1536], P('seq'), may hold values from -0.109375 to 0.109375
- halves: int32 [1, 128, 3, 2, 2], P('parts', 'seq'), may hold values from 1 to 3
Outputs:
- mixed: bfloat16 [1, 128, 3, 128, 1536], P('parts', 'seq')
The draws below stay inside these ranges and needn't reach their ends.
Inputs may be any that keep to these rules, and one draw needn't show every extreme that they name: `halves`: 1 lists the first half of the partner lines, 2 the second half, 3 both.
All inputs are finite; a program needn't handle non-finite values.
Results may differ from the reference program's by a relative error of at most 0.012.
Values may be sent and summed in bfloat16 or wider, within the bound.
A program may use at most 128 MiB of HBM per device.

```python
import math
import jax
import jax.numpy as jnp
from jax import lax

D = 3072
HEADS = 12
HDIM = 128
RES = 128
SCENES = 1
HW = 1536


def draw_queries(key, part):
    full_shape = (SCENES, RES, 3, RES, HEADS * HDIM)
    key_values = jax.random.fold_in(key, 0)
    drawn = jnp.clip(jax.random.normal(key_values, full_shape, jnp.float32), -6.0, 6.0)
    return drawn.astype(jnp.bfloat16)


def place_ends(result, rng, smallest, high):
    longest = result.shape.index(max(result.shape))
    spots = []
    for shift in (0, 1):
        where = [jax.random.randint(jax.random.fold_in(rng, axis), (), 0, length) for axis, length in enumerate(result.shape)]
        where[longest] = (where[longest] + shift) % result.shape[longest]
        spots.append(tuple(where))
    return result.at[spots[0]].set(smallest).at[spots[1]].set(high)


def shard_levels(own_key, shape, pieces, least, high):
    loudness, own = 1.0, jax.random.fold_in(own_key, 6)
    for position, blocks in pieces:
        steps = jnp.exp(jax.random.uniform(jax.random.fold_in(own, position), (blocks,), jnp.float32, least / len(pieces), high / len(pieces)))
        loudness = loudness * jnp.repeat(steps, shape[position] // blocks).reshape([-1 if axis == position else 1 for axis in range(len(shape))])
    return loudness


def scatter_about(rng, dims, spread, bound, cuts=(), kind=jnp.bfloat16):
    entries = spread * jax.random.normal(rng, dims, jnp.float32)
    if cuts:
        entries = entries * shard_levels(rng, dims, cuts, -0.22, 0.18)
    return jnp.clip(entries, -bound, bound).astype(kind)


def setup_inputs(seed: int = 0, part: int = 0) -> dict:
    key_of = jax.random.split(jax.random.key(seed), 6)
    part_splits = jax.random.split(jax.random.fold_in(key_of[5], part), 6)
    tokens = scatter_about(part_splits[0], (SCENES, RES, 3, RES, D), 1.0, 6.0, ((1, 32),))
    queries = draw_queries(jax.random.fold_in(jax.random.fold_in(key_of[5], part), 71), part)
    key_weight = scatter_about(key_of[2], (D, HW), D ** -0.5, 0.109375, ((0, 32),))
    value_weight = scatter_about(key_of[3], (D, HW), D ** -0.5, 0.109375, ((0, 32),))
    halves = place_ends(jax.random.randint(part_splits[4], (SCENES, RES, 3, 2, 2), 1, 4), jax.random.fold_in(part_splits[4], 1), 1, 3).astype(jnp.int32)
    return {"tokens": tokens, "queries": queries, "key_weight": key_weight, "value_weight": value_weight, "halves": halves}


def kept_keys(code_grid):
    column = jnp.arange(RES)
    first_kept = (code_grid % 2 == 1)[..., None]
    second_kept = (code_grid >= 2)[..., None]
    return jnp.where(column < RES // 2, first_kept, second_kept)[..., None, :]

def partial_attention(queries_h, keys_h, values_h, score_form, value_form, kept_mask):
    scores = jnp.einsum(score_form, queries_h, keys_h) * (1.0 / math.sqrt(HDIM))
    masked = jnp.where(kept_mask, scores, -jnp.inf)
    peak_val = lax.optimization_barrier(jnp.max(masked, axis=-1))
    weights = jnp.exp(masked - peak_val[..., None])
    totals = lax.optimization_barrier(jnp.sum(weights, axis=-1))
    rounded = lax.optimization_barrier(weights.astype(jnp.bfloat16)).astype(jnp.float32)
    partial_out = jnp.einsum(value_form, rounded, values_h)
    return (partial_out, peak_val, totals)

def merge_slots(near_part, far_part):
    far_mean = lax.optimization_barrier((far_part[0] / far_part[2][..., None]).astype(jnp.bfloat16)).astype(jnp.float32)
    peak_val = jnp.maximum(near_part[1], far_part[1])
    near_w = jnp.exp(near_part[1] - peak_val)
    far_w = jnp.exp(far_part[1] - peak_val) * far_part[2]
    upper = near_part[0] * near_w[..., None] + far_mean * far_w[..., None]
    return upper / (near_part[2] * near_w + far_w)[..., None]

def reference(tokens, queries, key_weight, value_weight, halves):
    half_index = jnp.arange(RES) // (RES // 2)
    slot_plan = (((1, 'abhd,ajhd->abhj', 'abhj,ajhd->abhd'), (2, 'abhd,bjhd->abhj', 'abhj,bjhd->abhd')), ((0, 'abhd,ajhd->abhj', 'abhj,ajhd->abhd'), (2, 'abhd,jbhd->abhj', 'abhj,jbhd->abhd')), ((0, 'abhd,jahd->abhj', 'abhj,jahd->abhd'), (1, 'abhd,jbhd->abhj', 'abhj,jbhd->abhd')))
    scene_outs = []
    for scene_idx in range(SCENES):
        flat_rows = tokens[scene_idx].reshape(-1, D)
        keys_all = jnp.dot(flat_rows, key_weight, preferred_element_type=jnp.float32).astype(jnp.bfloat16)
        keys_all = keys_all.reshape(RES, 3, RES, HEADS, HDIM).astype(jnp.float32)
        values_all = jnp.dot(flat_rows, value_weight, preferred_element_type=jnp.float32).astype(jnp.bfloat16)
        values_all = values_all.reshape(RES, 3, RES, HEADS, HDIM).astype(jnp.float32)
        query_all = queries[scene_idx].reshape(RES, 3, RES, HEADS, HDIM).astype(jnp.float32)
        plane_outs = []
        for plane_idx in range(3):
            results = []
            for slot_idx in range(2):
                source_idx, score_form, value_form = slot_plan[plane_idx][slot_idx]
                code_pairs = halves[scene_idx, :, plane_idx, :, slot_idx]
                code_grid = jnp.where(half_index[None, :] == 0, code_pairs[:, 0:1], code_pairs[:, 1:2])
                results.append(partial_attention(query_all[:, plane_idx], keys_all[:, source_idx], values_all[:, source_idx], score_form, value_form, kept_keys(code_grid)))
            merged = merge_slots(results[0], results[1])
            plane_outs.append(merged.reshape(RES, RES, HEADS * HDIM))
        scene_outs.append(jnp.stack(plane_outs, axis=1).astype(jnp.bfloat16))
    return jnp.stack(scene_outs, axis=0)
```

```python
import functools
import math

import jax
import jax.numpy as jnp
from jax import lax
from jax.experimental import pallas as pl
from jax.experimental.pallas import tpu as pltpu
from jax.sharding import PartitionSpec as P

HDIM = 128
LANES = 128
MESH = pl.DeviceIdType.MESH


def fold(pos, ring):
    return pos + (pos // (ring // 2)) * (3 * ring // 2 - 1 - 2 * pos)


def gather_kernel(lines, ring, code_in, key_in, value_in, code_out, key_out, value_out, own_sem, send_sem, recv_sem):
    ins = (code_in, key_in, value_in)
    outs = (code_out, key_out, value_out)
    me = lax.axis_index("seq")
    chip, core = me // 2, me % 2
    z, pos = chip // ring, fold(chip % ring, ring)
    sibling = me + 1 - 2 * core

    def index(zz, pp):
        return (zz * ring + fold((pp + ring) % ring, ring)) * 2 + core

    up, down = index(z + 1, pos), index(z - 1, pos)
    right, left = index(z, pos + 1), index(z, pos - 1)

    barrier = pltpu.get_barrier_semaphore()
    for dev in (sibling, right, left):
        pl.semaphore_signal(barrier, inc=1, device_id={"seq": dev}, device_id_type=MESH)

    @pl.when(z + 1 < lines)
    def _():
        pl.semaphore_signal(barrier, inc=1, device_id={"seq": up}, device_id_type=MESH)

    @pl.when(z >= 1)
    def _():
        pl.semaphore_signal(barrier, inc=1, device_id={"seq": down}, device_id_type=MESH)

    has_up, has_down = 1 - (z + 1) // lines, (z + lines - 1) // lines
    pl.semaphore_wait(barrier, 3 + has_up + has_down)

    kinds = range(3)
    locals_ = [pltpu.make_async_copy(ins[t], outs[t].at[me], own_sem.at[t]) for t in kinds]
    for copy in locals_:
        copy.start()
    sent = []

    def make(t, slot, way, dev, own):
        return pltpu.make_async_remote_copy(
            src_ref=ins[t] if own else outs[t].at[slot],
            dst_ref=outs[t].at[slot],
            send_sem=send_sem.at[t, slot // 2, way],
            recv_sem=recv_sem.at[t, slot],
            device_id={"seq": dev},
            device_id_type=MESH,
        )

    def guarded(cond, work):
        if cond is None:
            work()
        else:
            pl.when(cond)(work)

    def send(cond, *what):
        sent.append((cond, what))
        guarded(cond, lambda: make(*what).start())

    def arrive(cond, t, slot):
        guarded(cond, lambda: make(t, slot, 0, sibling, False).wait_recv())

    def sources(dz):
        if dz == 0:
            return ((z, None, 0),)
        return ((z + dz, z + dz < lines, 1), (z - dz, z >= dz, -1))

    def both(one, two):
        return two if one is None else jnp.logical_and(one, two)

    def line_stage(dz):
        for t in kinds:
            for zz, cond, sign in sources(dz):
                slot = index(zz, pos)
                own = dz == 0
                if not own:
                    arrive(cond, t, slot)
                if sign >= 0:
                    send(both(cond, z >= 1), t, slot, 0, down, own)
                if sign <= 0:
                    send(both(cond, z + 1 < lines), t, slot, 1, up, own)
                send(cond, t, slot, 2, right, own)
                send(cond, t, slot, 3, left, own)
                send(cond, t, slot, 4, sibling, own)

    def ring_stage(dz):
        for step in range(1, ring // 2 + 1):
            for t in kinds:
                far, near = ring // 2, (ring - 1) // 2
                to_right, to_left = (near, far) if t == 2 else (far, near)
                for zz, cond, _ in sources(dz):
                    if step <= to_right:
                        slot = index(zz, pos - step)
                        arrive(cond, t, slot)
                        if step < to_right:
                            send(cond, t, slot, 2, right, False)
                        send(cond, t, slot, 4, sibling, False)
                    if step <= to_left:
                        slot = index(zz, pos + step)
                        arrive(cond, t, slot)
                        if step < to_left:
                            send(cond, t, slot, 3, left, False)
                        send(cond, t, slot, 4, sibling, False)

    for dz in range(lines + 1):
        if dz < lines:
            line_stage(dz)
        if dz >= 1:
            ring_stage(dz - 1)
    for t in kinds:
        for chip_slot in range(lines * ring):
            arrive(None, t, chip_slot * 2 + 1 - core)
    for cond, what in sent:
        guarded(cond, lambda what=what: make(*what).wait_send())
    for copy in locals_:
        copy.wait()


def gather_all(size, codes, key_weight, value_weight):
    side = math.isqrt(size // 2)
    if size % 2 or 2 * side * side != size or side < 4 or side % 2:
        return tuple(lax.all_gather(x, "seq", axis=0) for x in (codes, key_weight, value_weight))
    ins = (codes, key_weight, value_weight)
    chips = side * side
    return pl.pallas_call(
        functools.partial(gather_kernel, side, side),
        out_shape=[jax.ShapeDtypeStruct((size,) + x.shape, x.dtype) for x in ins],
        in_specs=[pl.BlockSpec(memory_space=pl.ANY)] * 3,
        out_specs=[pl.BlockSpec(memory_space=pl.ANY)] * 3,
        scratch_shapes=[
            pltpu.SemaphoreType.DMA((3,)),
            pltpu.SemaphoreType.DMA((3, chips, 5)),
            pltpu.SemaphoreType.DMA((3, size)),
        ],
        compiler_params=pltpu.CompilerParams(collective_id=0, has_side_effects=True),
        cost_estimate=pl.CostEstimate(flops=8 * 10**10, bytes_accessed=2 * 10**7, transcendentals=0),
        name="gather_weights",
    )(*ins)


def one_slot(q_ref, k_ref, v_ref, bias, head):
    cols = pl.ds(head * HDIM, HDIM)
    scores = lax.dot_general(
        q_ref[0, 0, :, cols], k_ref[0, 0, :, cols], (((1,), (1,)), ((), ())), preferred_element_type=jnp.float32
    ) * (1.0 / math.sqrt(HDIM)) + bias
    peak = jnp.max(scores, axis=-1, keepdims=True)
    weights = jnp.exp(scores - peak)
    total = jnp.sum(weights, axis=-1, keepdims=True)
    partial = jnp.dot(weights.astype(jnp.bfloat16), v_ref[0, 0, :, cols], preferred_element_type=jnp.float32)
    return partial, peak, total


def three_parts(value):
    parts = []
    for _ in range(3):
        part = value.astype(jnp.bfloat16).astype(jnp.float32)
        parts.append(part)
        value = value - part
    return parts


def far_kernel(heads, q_ref, k_ref, v_ref, bias_ref, out_ref):
    bias = bias_ref[0]
    lane = lax.broadcasted_iota(jnp.int32, (bias.shape[0], LANES), 1)
    stats = jnp.zeros(lane.shape, jnp.float32)
    for head in range(heads):
        partial, peak, total = one_slot(q_ref, k_ref, v_ref, bias, head)
        out_ref[0, 0, :, pl.ds(head * HDIM, HDIM)] = (partial / total).astype(jnp.bfloat16)
        for at, part in enumerate(three_parts(peak) + three_parts(total)):
            stats = jnp.where(lane == 6 * head + at, part, stats)
    out_ref[0, 0, :, pl.ds(heads * HDIM, LANES)] = stats.astype(jnp.bfloat16)


def near_kernel(heads, q_ref, k_ref, v_ref, bias_ref, back_ref, *rest):
    out_ref = rest[-1]
    bias = bias_ref[0]
    stats = back_ref[0, 0, :, pl.ds(heads * HDIM, LANES)].astype(jnp.float32)
    for head in range(heads):
        cols = pl.ds(head * HDIM, HDIM)
        partial, peak, total = one_slot(q_ref, k_ref, v_ref, bias, head)
        col = [stats[:, 6 * head + at : 6 * head + at + 1] for at in range(6)]
        far_peak = col[0] + col[1] + col[2]
        far_total = col[3] + col[4] + col[5]
        top = jnp.maximum(peak, far_peak)
        near_w = jnp.exp(peak - top)
        far_w = jnp.exp(far_peak - top) * far_total
        upper = partial * near_w + back_ref[0, 0, :, cols].astype(jnp.float32) * far_w
        out_ref[0, 0, :, cols] = (upper / (total * near_w + far_w)).astype(jnp.bfloat16)


def plane_spec(array, plane):
    return pl.BlockSpec((1, 1) + array.shape[2:], lambda g: (g, plane, 0, 0))


def attend_cost(groups, rows, keys, width):
    return pl.CostEstimate(
        flops=40 * groups * rows * keys * width, bytes_accessed=8 * groups * rows * width, transcendentals=0
    )


def far_part(operands, bias):
    groups, rows, keys = bias.shape
    width = operands[0][0].shape[-1]
    return pl.pallas_call(
        functools.partial(far_kernel, width // HDIM),
        grid=(groups,),
        in_specs=[plane_spec(a, p) for a, p in operands] + [pl.BlockSpec((1, rows, keys), lambda g: (g, 0, 0))],
        out_specs=pl.BlockSpec((1, 1, rows, width + LANES), lambda g: (g, 0, 0, 0)),
        out_shape=jax.ShapeDtypeStruct((groups, 1, rows, width + LANES), jnp.bfloat16),
        cost_estimate=attend_cost(groups, rows, keys, width),
        name="far_slot",
    )(*[a for a, _ in operands], bias)


def near_part(operands, bias, back, plane, planes, so_far):
    groups, rows, keys = bias.shape
    width = operands[0][0].shape[-1]
    in_specs = [plane_spec(a, p) for a, p in operands]
    in_specs += [pl.BlockSpec((1, rows, keys), lambda g: (g, 0, 0)), plane_spec(back, 0)]
    args = [a for a, _ in operands] + [bias, back]
    aliases = {}
    if so_far is not None:
        in_specs.append(pl.BlockSpec(memory_space=pl.ANY))
        args.append(so_far)
        aliases = {len(args) - 1: 0}
    return pl.pallas_call(
        functools.partial(near_kernel, width // HDIM),
        grid=(groups,),
        in_specs=in_specs,
        out_specs=pl.BlockSpec((1, 1, rows, width), lambda g: (g, plane, 0, 0)),
        out_shape=jax.ShapeDtypeStruct((groups, planes, rows, width), jnp.bfloat16),
        input_output_aliases=aliases,
        cost_estimate=attend_cost(groups, rows, keys, width),
        name="near_slot",
    )(*args)


def swap_lines(array, scenes, size):
    groups, planes, positions, width = array.shape
    lines, own = groups // scenes, positions // size
    cut = array.reshape(scenes, lines, planes, size, own, width).transpose(3, 0, 2, 4, 1, 5)
    got = lax.all_to_all(cut, "seq", split_axis=0, concat_axis=0, tiled=True)
    got = got.transpose(1, 3, 2, 0, 4, 5)
    return got.reshape(scenes * own, planes, size * lines, width)


def keep_bias(codes, keys):
    column = jnp.arange(keys)
    kept = jnp.where(column < keys // 2, (codes % 2 == 1)[..., None], (codes >= 2)[..., None])
    return jnp.where(kept, 0.0, -jnp.inf).astype(jnp.float32)


def on_device(size, tokens, queries, key_weight, value_weight, halves):
    scenes, lines, planes, positions, depth = tokens.shape
    width = queries.shape[-1]
    groups = scenes * lines
    q_home = queries.reshape(groups, planes, positions, width)
    swap = functools.partial(swap_lines, scenes=scenes, size=size)

    flat_codes = halves.reshape(-1)
    padded = -(-flat_codes.size // (8 * LANES)) * 8 * LANES
    code_tile = jnp.pad(flat_codes, (0, padded - flat_codes.size)).reshape(-1, LANES)
    code_all, key_all, value_all = gather_all(size, code_tile, key_weight, value_weight)
    code_all = code_all.reshape(size, -1)[:, : flat_codes.size].reshape((size,) + halves.shape)
    code_all = jnp.moveaxis(code_all, 0, 1).reshape(scenes, size * lines, planes, 2, 2)

    q_moved = swap(q_home)

    home_rows = tokens.reshape(-1, depth)
    home_shape = (groups, planes, positions, width)
    keys = jnp.dot(home_rows, key_all.reshape(depth, width), preferred_element_type=jnp.float32)
    keys = keys.astype(jnp.bfloat16).reshape(home_shape)
    values = jnp.dot(home_rows, value_all.reshape(depth, width), preferred_element_type=jnp.float32)
    values = values.astype(jnp.bfloat16).reshape(home_shape)

    keys, values, q_moved = lax.optimization_barrier((keys, values, q_moved))
    k2, v2 = swap(keys[:, 2:]), swap(values[:, 2:])
    k1, v1 = swap(keys[:, 1:2]), swap(values[:, 1:2])
    k0, v0 = swap(keys[:, :1]), swap(values[:, :1])

    own = positions // size
    own_half = (lax.axis_index("seq") * own + jnp.arange(own)) // (positions // 2)
    home_half = jnp.arange(positions) // (positions // 2)

    def far_bias(plane):
        pairs = code_all[:, None, :, plane, :, 1]
        codes = jnp.where(own_half[None, :, None] == 0, pairs[..., 0], pairs[..., 1])
        return keep_bias(codes.reshape(scenes * own, size * lines), size * lines)

    def near_bias(plane):
        pairs = halves[:, :, plane, :, 0].reshape(groups, 1, 2)
        codes = jnp.where(home_half[None, :] == 0, pairs[..., 0], pairs[..., 1])
        return keep_bias(codes, positions)

    def back(far):
        return swap_lines(far, scenes, size)

    back0 = back(far_part(((q_moved, 0), (keys, 2), (values, 2)), far_bias(0)))
    back1 = back(far_part(((q_moved, 1), (k2, 0), (v2, 0)), far_bias(1)))
    back2 = back(far_part(((q_moved, 2), (k1, 0), (v1, 0)), far_bias(2)))

    out = near_part(((q_home, 0), (keys, 1), (values, 1)), near_bias(0), back0, 0, planes, None)
    out = near_part(((q_home, 1), (keys, 0), (values, 0)), near_bias(1), back1, 1, planes, out)
    out = near_part(((q_home, 2), (k0, 0), (v0, 0)), near_bias(2), back2, 2, planes, out)
    return out.reshape(queries.shape)


def solution(mesh):
    lines = P("parts", "seq", None, None, None)
    rows = P("seq", None)
    return jax.shard_map(
        functools.partial(on_device, mesh.shape["seq"]),
        mesh=mesh,
        in_specs=(lines, lines, rows, rows, lines),
        out_specs=lines,
        check_vma=False,
    )
```

```python
import functools
import math

import jax
import jax.numpy as jnp
from jax import lax
from jax.experimental import pallas as pl
from jax.experimental.pallas import tpu as pltpu
from jax.sharding import PartitionSpec as P

HDIM = 128
LANES = 128
MESH = pl.DeviceIdType.MESH


def fold(pos, ring):
    return pos + (pos // (ring // 2)) * (3 * ring // 2 - 1 - 2 * pos)


def gather_kernel(lines, ring, code_in, key_in, value_in, code_out, key_out, value_out, own_sem, send_sem, recv_sem):
    ins = (code_in, key_in, value_in)
    outs = (code_out, key_out, value_out)
    me = lax.axis_index("seq")
    chip, core = me // 2, me % 2
    z, pos = chip // ring, fold(chip % ring, ring)
    sibling = me + 1 - 2 * core

    def index(zz, pp):
        return (zz * ring + fold((pp + ring) % ring, ring)) * 2 + core

    up, down = index(z + 1, pos), index(z - 1, pos)
    right, left = index(z, pos + 1), index(z, pos - 1)

    barrier = pltpu.get_barrier_semaphore()
    for dev in (sibling, right, left):
        pl.semaphore_signal(barrier, inc=1, device_id={"seq": dev}, device_id_type=MESH)

    @pl.when(z + 1 < lines)
    def _():
        pl.semaphore_signal(barrier, inc=1, device_id={"seq": up}, device_id_type=MESH)

    @pl.when(z >= 1)
    def _():
        pl.semaphore_signal(barrier, inc=1, device_id={"seq": down}, device_id_type=MESH)

    has_up, has_down = 1 - (z + 1) // lines, (z + lines - 1) // lines
    pl.semaphore_wait(barrier, 3 + has_up + has_down)

    kinds = range(3)
    locals_ = [pltpu.make_async_copy(ins[t], outs[t].at[me], own_sem.at[t]) for t in kinds]
    for copy in locals_:
        copy.start()
    sent = []

    def make(t, slot, way, dev, own):
        return pltpu.make_async_remote_copy(
            src_ref=ins[t] if own else outs[t].at[slot],
            dst_ref=outs[t].at[slot],
            send_sem=send_sem.at[t, slot // 2, way],
            recv_sem=recv_sem.at[t, slot],
            device_id={"seq": dev},
            device_id_type=MESH,
        )

    def guarded(cond, work):
        if cond is None:
            work()
        else:
            pl.when(cond)(work)

    def send(cond, *what):
        sent.append((cond, what))
        guarded(cond, lambda: make(*what).start())

    def arrive(cond, t, slot):
        guarded(cond, lambda: make(t, slot, 0, sibling, False).wait_recv())

    def sources(dz):
        if dz == 0:
            return ((z, None, 0),)
        return ((z + dz, z + dz < lines, 1), (z - dz, z >= dz, -1))

    def both(one, two):
        return two if one is None else jnp.logical_and(one, two)

    def line_stage(dz):
        for t in kinds:
            for zz, cond, sign in sources(dz):
                slot = index(zz, pos)
                own = dz == 0
                if not own:
                    arrive(cond, t, slot)
                if sign >= 0:
                    send(both(cond, z >= 1), t, slot, 0, down, own)
                if sign <= 0:
                    send(both(cond, z + 1 < lines), t, slot, 1, up, own)
                send(cond, t, slot, 2, right, own)
                send(cond, t, slot, 3, left, own)
                send(cond, t, slot, 4, sibling, own)

    def ring_stage(dz):
        for step in range(1, ring // 2 + 1):
            for t in kinds:
                far, near = ring // 2, (ring - 1) // 2
                to_right, to_left = (near, far) if t == 2 else (far, near)
                for zz, cond, _ in sources(dz):
                    if step <= to_right:
                        slot = index(zz, pos - step)
                        arrive(cond, t, slot)
                        if step < to_right:
                            send(cond, t, slot, 2, right, False)
                        send(cond, t, slot, 4, sibling, False)
                    if step <= to_left:
                        slot = index(zz, pos + step)
                        arrive(cond, t, slot)
                        if step < to_left:
                            send(cond, t, slot, 3, left, False)
                        send(cond, t, slot, 4, sibling, False)

    for dz in range(lines + 1):
        if dz < lines:
            line_stage(dz)
        if dz >= 1:
            ring_stage(dz - 1)
    for t in kinds:
        for chip_slot in range(lines * ring):
            arrive(None, t, chip_slot * 2 + 1 - core)
    for cond, what in sent:
        guarded(cond, lambda what=what: make(*what).wait_send())
    for copy in locals_:
        copy.wait()


def gather_all(size, codes, key_weight, value_weight):
    side = math.isqrt(size // 2)
    if size % 2 or 2 * side * side != size or side < 4 or side % 2:
        return tuple(lax.all_gather(x, "seq", axis=0) for x in (codes, key_weight, value_weight))
    ins = (codes, key_weight, value_weight)
    chips = side * side
    return pl.pallas_call(
        functools.partial(gather_kernel, side, side),
        out_shape=[jax.ShapeDtypeStruct((size,) + x.shape, x.dtype) for x in ins],
        in_specs=[pl.BlockSpec(memory_space=pl.ANY)] * 3,
        out_specs=[pl.BlockSpec(memory_space=pl.ANY)] * 3,
        scratch_shapes=[
            pltpu.SemaphoreType.DMA((3,)),
            pltpu.SemaphoreType.DMA((3, chips, 5)),
            pltpu.SemaphoreType.DMA((3, size)),
        ],
        compiler_params=pltpu.CompilerParams(collective_id=0, has_side_effects=True),
        cost_estimate=pl.CostEstimate(flops=8 * 10**10, bytes_accessed=2 * 10**7, transcendentals=0),
        name="gather_weights",
    )(*ins)


def one_slot(q_ref, k_ref, v_ref, bias, head):
    cols = pl.ds(head * HDIM, HDIM)
    scores = lax.dot_general(
        q_ref[0, 0, :, cols], k_ref[0, 0, :, cols], (((1,), (1,)), ((), ())), preferred_element_type=jnp.float32
    ) * (1.0 / math.sqrt(HDIM)) + bias
    peak = jnp.max(scores, axis=-1, keepdims=True)
    weights = jnp.exp(scores - peak)
    total = jnp.sum(weights, axis=-1, keepdims=True)
    partial = jnp.dot(weights.astype(jnp.bfloat16), v_ref[0, 0, :, cols], preferred_element_type=jnp.float32)
    return partial, peak, total


def three_parts(value):
    parts = []
    for _ in range(3):
        part = value.astype(jnp.bfloat16).astype(jnp.float32)
        parts.append(part)
        value = value - part
    return parts


def far_kernel(heads, q_ref, k_ref, v_ref, bias_ref, out_ref):
    bias = bias_ref[0]
    lane = lax.broadcasted_iota(jnp.int32, (bias.shape[0], LANES), 1)
    stats = jnp.zeros(lane.shape, jnp.float32)
    for head in range(heads):
        partial, peak, total = one_slot(q_ref, k_ref, v_ref, bias, head)
        out_ref[0, 0, :, pl.ds(head * HDIM, HDIM)] = (partial / total).astype(out_ref.dtype)
        for at, part in enumerate(three_parts(peak) + three_parts(total)):
            stats = jnp.where(lane == at * heads + head, part, stats)
    out_ref[0, 0, :, pl.ds(heads * HDIM, LANES)] = stats.astype(out_ref.dtype)


def read_stats(ref, heads):
    stats = ref[0, 0, :, pl.ds(heads * HDIM, LANES)].astype(jnp.float32)
    parts = [stats[:, at * heads : (at + 1) * heads] for at in range(6)]
    return parts[0] + parts[1] + parts[2], parts[3] + parts[4] + parts[5]


def merge_kernel(heads, near_ref, back_ref, so_far_ref, out_ref):
    near_peak, near_total = read_stats(near_ref, heads)
    far_peak, far_total = read_stats(back_ref, heads)
    top = jnp.maximum(near_peak, far_peak)
    near_w = near_total * jnp.exp(near_peak - top)
    far_w = far_total * jnp.exp(far_peak - top)
    scale = 1.0 / (near_w + far_w)
    near_w, far_w = near_w * scale, far_w * scale
    for head in range(heads):
        cols = pl.ds(head * HDIM, HDIM)
        mixed = near_ref[0, 0, :, cols] * near_w[:, head : head + 1]
        mixed += back_ref[0, 0, :, cols].astype(jnp.float32) * far_w[:, head : head + 1]
        out_ref[0, 0, :, cols] = mixed.astype(jnp.bfloat16)


def near_kernel(heads, q_ref, k_ref, v_ref, bias_ref, back_ref, *rest):
    out_ref = rest[-1]
    bias = bias_ref[0]
    far_peaks, far_totals = read_stats(back_ref, heads)
    for head in range(heads):
        cols = pl.ds(head * HDIM, HDIM)
        partial, peak, total = one_slot(q_ref, k_ref, v_ref, bias, head)
        far_peak, far_total = far_peaks[:, head : head + 1], far_totals[:, head : head + 1]
        top = jnp.maximum(peak, far_peak)
        near_w = jnp.exp(peak - top)
        far_w = jnp.exp(far_peak - top) * far_total
        upper = partial * near_w + back_ref[0, 0, :, cols].astype(jnp.float32) * far_w
        out_ref[0, 0, :, cols] = (upper / (total * near_w + far_w)).astype(jnp.bfloat16)


def plane_spec(array, plane):
    return pl.BlockSpec((1, 1) + array.shape[2:], lambda g: (g, plane, 0, 0))


def attend_cost(groups, rows, keys, width):
    return pl.CostEstimate(
        flops=150 * groups * rows * keys * width, bytes_accessed=8 * groups * rows * width, transcendentals=0
    )


def far_part(operands, bias, kind=jnp.bfloat16):
    groups, rows, keys = bias.shape
    width = operands[0][0].shape[-1]
    return pl.pallas_call(
        functools.partial(far_kernel, width // HDIM),
        grid=(groups,),
        in_specs=[plane_spec(a, p) for a, p in operands] + [pl.BlockSpec((1, rows, keys), lambda g: (g, 0, 0))],
        out_specs=pl.BlockSpec((1, 1, rows, width + LANES), lambda g: (g, 0, 0, 0)),
        out_shape=jax.ShapeDtypeStruct((groups, 1, rows, width + LANES), kind),
        cost_estimate=attend_cost(groups, rows, keys, width),
        name="far_slot",
    )(*[a for a, _ in operands], bias)


def near_part(operands, bias, back, back_plane, plane, planes, so_far):
    groups, rows, keys = bias.shape
    width = operands[0][0].shape[-1]
    in_specs = [plane_spec(a, p) for a, p in operands]
    in_specs += [pl.BlockSpec((1, rows, keys), lambda g: (g, 0, 0)), plane_spec(back, back_plane)]
    args = [a for a, _ in operands] + [bias, back]
    aliases = {}
    if so_far is not None:
        in_specs.append(pl.BlockSpec(memory_space=pl.ANY))
        args.append(so_far)
        aliases = {len(args) - 1: 0}
    return pl.pallas_call(
        functools.partial(near_kernel, width // HDIM),
        grid=(groups,),
        in_specs=in_specs,
        out_specs=pl.BlockSpec((1, 1, rows, width), lambda g: (g, plane, 0, 0)),
        out_shape=jax.ShapeDtypeStruct((groups, planes, rows, width), jnp.bfloat16),
        input_output_aliases=aliases,
        cost_estimate=attend_cost(groups, rows, keys, width),
        name="near_slot",
    )(*args)


def merge_part(near, back, plane, so_far):
    groups, planes, rows, width = so_far.shape
    return pl.pallas_call(
        functools.partial(merge_kernel, width // HDIM),
        grid=(groups,),
        in_specs=[plane_spec(near, 0), plane_spec(back, 0), pl.BlockSpec(memory_space=pl.ANY)],
        out_specs=pl.BlockSpec((1, 1, rows, width), lambda g: (g, plane, 0, 0)),
        out_shape=jax.ShapeDtypeStruct(so_far.shape, so_far.dtype),
        input_output_aliases={2: 0},
        name="merge_slots",
    )(near, back, so_far)


def cut_lines(array, scenes, size):
    groups, planes, positions, width = array.shape
    lines, own = groups // scenes, positions // size
    return array.reshape(scenes, lines, planes, size, own, width).transpose(3, 0, 2, 4, 1, 5)


def swap_cut(cut):
    got = lax.all_to_all(cut, "seq", split_axis=0, concat_axis=0, tiled=True)
    return got, got.transpose(1, 3, 2, 0, 4, 5)


def keep_bias(codes, keys):
    column = jnp.arange(keys)
    kept = jnp.where(column < keys // 2, (codes % 2 == 1)[..., None], (codes >= 2)[..., None])
    return jnp.where(kept, 0.0, -jnp.inf).astype(jnp.float32)


def on_device(size, tokens, queries, key_weight, value_weight, halves):
    scenes, lines, planes, positions, depth = tokens.shape
    width = queries.shape[-1]
    groups = scenes * lines
    q_home = queries.reshape(groups, planes, positions, width)

    def cut(*arrays):
        return jnp.concatenate([cut_lines(a, scenes, size) for a in arrays], axis=2)

    def swap(blocks, *after):
        blocks = lax.optimization_barrier((blocks,) + after)[0]
        got, turned = swap_cut(blocks)
        return got, turned.reshape(-1, turned.shape[2], size * turned.shape[4], turned.shape[5])

    flat_codes = halves.reshape(-1)
    padded = -(-flat_codes.size // (8 * LANES)) * 8 * LANES
    code_tile = jnp.pad(flat_codes, (0, padded - flat_codes.size)).reshape(-1, LANES)
    code_all, key_all, value_all = gather_all(size, code_tile, key_weight, value_weight)
    code_all = code_all.reshape(size, -1)[:, : flat_codes.size].reshape((size,) + halves.shape)
    code_all = jnp.moveaxis(code_all, 0, 1).reshape(scenes, size * lines, planes, 2, 2)

    q0_got, q0 = swap(cut(q_home[:, :1]))
    q12_got, q12 = swap(cut(q_home[:, 1:]), key_all)

    home_rows = tokens.reshape(-1, depth)
    home_shape = (groups, planes, positions, width)
    keys = jnp.dot(home_rows, key_all.reshape(depth, width), preferred_element_type=jnp.float32)
    keys = keys.astype(jnp.bfloat16).reshape(home_shape)
    values = jnp.dot(home_rows, value_all.reshape(depth, width), preferred_element_type=jnp.float32)
    values = values.astype(jnp.bfloat16).reshape(home_shape)

    own = positions // size
    own_half = (lax.axis_index("seq") * own + jnp.arange(own)) // (positions // 2)
    home_half = jnp.arange(positions) // (positions // 2)

    def far_bias(plane):
        pairs = code_all[:, None, :, plane, :, 1]
        codes = jnp.where(own_half[None, :, None] == 0, pairs[..., 0], pairs[..., 1])
        return keep_bias(codes.reshape(scenes * own, size * lines), size * lines)

    def near_bias(plane):
        pairs = halves[:, :, plane, :, 0].reshape(groups, 1, 2)
        codes = jnp.where(home_half[None, :] == 0, pairs[..., 0], pairs[..., 1])
        return keep_bias(codes, positions)

    kv2_got, kv2 = swap(cut(keys[:, 2:], values[:, 2:]), q0_got, q12_got)
    kv1_got, kv1 = swap(cut(keys[:, 1:2], values[:, 1:2]), kv2_got)
    far0 = far_part(((q0, 0), (keys, 2), (values, 2)), far_bias(0))
    far1 = far_part(((q12, 0), (kv2, 0), (kv2, 1)), far_bias(1))
    back01_got, back01 = swap(cut(far0, far1), kv1_got)
    kv0_got, kv0 = swap(cut(keys[:, :1], values[:, :1]), back01_got)
    far2 = far_part(((q12, 1), (kv1, 0), (kv1, 1)), far_bias(2))
    _, back2 = swap(cut(far2), kv0_got)

    out = near_part(((q_home, 0), (keys, 1), (values, 1)), near_bias(0), back01, 0, 0, planes, None)
    out = near_part(((q_home, 1), (keys, 0), (values, 0)), near_bias(1), back01, 1, 1, planes, out)
    near2 = far_part(((q_home, 2), (kv0, 0), (kv0, 1)), near_bias(2), jnp.float32)
    out = merge_part(near2, back2, 2, out)
    return out.reshape(queries.shape)


def solution(mesh):
    lines = P("parts", "seq", None, None, None)
    rows = P("seq", None)
    return jax.shard_map(
        functools.partial(on_device, mesh.shape["seq"]),
        mesh=mesh,
        in_specs=(lines, lines, rows, rows, lines),
        out_specs=lines,
        check_vma=False,
    )
```

```python
import functools
import math

import jax
import jax.numpy as jnp
from jax import lax
from jax.experimental import pallas as pl
from jax.experimental.pallas import tpu as pltpu
from jax.sharding import PartitionSpec as P

HDIM = 128
LANES = 128
MESH = pl.DeviceIdType.MESH


def fold(pos, ring):
    return pos + (pos // (ring // 2)) * (3 * ring // 2 - 1 - 2 * pos)


def gather_kernel(lines, ring, code_in, key_in, value_in, code_out, key_out, value_out, own_sem, send_sem, recv_sem):
    ins = (code_in, key_in, value_in)
    outs = (code_out, key_out, value_out)
    me = lax.axis_index("seq")
    chip, core = me // 2, me % 2
    z, pos = chip // ring, fold(chip % ring, ring)
    sibling = me + 1 - 2 * core

    def index(zz, pp):
        return (zz * ring + fold((pp + ring) % ring, ring)) * 2 + core

    up, down = index(z + 1, pos), index(z - 1, pos)
    right, left = index(z, pos + 1), index(z, pos - 1)

    barrier = pltpu.get_barrier_semaphore()
    for dev in (sibling, right, left):
        pl.semaphore_signal(barrier, inc=1, device_id={"seq": dev}, device_id_type=MESH)

    @pl.when(z + 1 < lines)
    def _():
        pl.semaphore_signal(barrier, inc=1, device_id={"seq": up}, device_id_type=MESH)

    @pl.when(z >= 1)
    def _():
        pl.semaphore_signal(barrier, inc=1, device_id={"seq": down}, device_id_type=MESH)

    has_up, has_down = 1 - (z + 1) // lines, (z + lines - 1) // lines
    pl.semaphore_wait(barrier, 3 + has_up + has_down)

    kinds = range(3)
    locals_ = [pltpu.make_async_copy(ins[t], outs[t].at[me], own_sem.at[t]) for t in kinds]
    for copy in locals_:
        copy.start()
    sent = []

    def make(t, slot, way, dev, own):
        return pltpu.make_async_remote_copy(
            src_ref=ins[t] if own else outs[t].at[slot],
            dst_ref=outs[t].at[slot],
            send_sem=send_sem.at[t, slot // 2, way],
            recv_sem=recv_sem.at[t, slot],
            device_id={"seq": dev},
            device_id_type=MESH,
        )

    def guarded(cond, work):
        if cond is None:
            work()
        else:
            pl.when(cond)(work)

    def send(cond, *what):
        sent.append((cond, what))
        guarded(cond, lambda: make(*what).start())

    def arrive(cond, t, slot):
        guarded(cond, lambda: make(t, slot, 0, sibling, False).wait_recv())

    def sources(dz):
        if dz == 0:
            return ((z, None, 0),)
        return ((z + dz, z + dz < lines, 1), (z - dz, z >= dz, -1))

    def both(one, two):
        return two if one is None else jnp.logical_and(one, two)

    def line_stage(dz):
        for t in kinds:
            for zz, cond, sign in sources(dz):
                slot = index(zz, pos)
                own = dz == 0
                if not own:
                    arrive(cond, t, slot)
                if sign >= 0:
                    send(both(cond, z >= 1), t, slot, 0, down, own)
                if sign <= 0:
                    send(both(cond, z + 1 < lines), t, slot, 1, up, own)
                send(cond, t, slot, 2, right, own)
                send(cond, t, slot, 3, left, own)
                send(cond, t, slot, 4, sibling, own)

    def ring_stage(dz):
        for step in range(1, ring // 2 + 1):
            for t in kinds:
                far, near = ring // 2, (ring - 1) // 2
                to_right, to_left = (near, far) if t == 2 else (far, near)
                for zz, cond, _ in sources(dz):
                    if step <= to_right:
                        slot = index(zz, pos - step)
                        arrive(cond, t, slot)
                        if step < to_right:
                            send(cond, t, slot, 2, right, False)
                        send(cond, t, slot, 4, sibling, False)
                    if step <= to_left:
                        slot = index(zz, pos + step)
                        arrive(cond, t, slot)
                        if step < to_left:
                            send(cond, t, slot, 3, left, False)
                        send(cond, t, slot, 4, sibling, False)

    for dz in range(lines + 1):
        if dz < lines:
            line_stage(dz)
        if dz >= 1:
            ring_stage(dz - 1)
    for t in kinds:
        for chip_slot in range(lines * ring):
            arrive(None, t, chip_slot * 2 + 1 - core)
    for cond, what in sent:
        guarded(cond, lambda what=what: make(*what).wait_send())
    for copy in locals_:
        copy.wait()


def gather_all(size, codes, key_weight, value_weight):
    side = math.isqrt(size // 2)
    if size % 2 or 2 * side * side != size or side < 4 or side % 2:
        return tuple(lax.all_gather(x, "seq", axis=0) for x in (codes, key_weight, value_weight))
    ins = (codes, key_weight, value_weight)
    chips = side * side
    return pl.pallas_call(
        functools.partial(gather_kernel, side, side),
        out_shape=[jax.ShapeDtypeStruct((size,) + x.shape, x.dtype) for x in ins],
        in_specs=[pl.BlockSpec(memory_space=pl.ANY)] * 3,
        out_specs=[pl.BlockSpec(memory_space=pl.ANY)] * 3,
        scratch_shapes=[
            pltpu.SemaphoreType.DMA((3,)),
            pltpu.SemaphoreType.DMA((3, chips, 5)),
            pltpu.SemaphoreType.DMA((3, size)),
        ],
        compiler_params=pltpu.CompilerParams(collective_id=0, has_side_effects=True),
        cost_estimate=pl.CostEstimate(flops=8 * 10**10, bytes_accessed=2 * 10**7, transcendentals=0),
        name="gather_weights",
    )(*ins)


def one_slot(q_ref, k_ref, v_ref, bias, head):
    cols = pl.ds(head * HDIM, HDIM)
    scores = lax.dot_general(
        q_ref[0, 0, :, cols], k_ref[0, 0, :, cols], (((1,), (1,)), ((), ())), preferred_element_type=jnp.float32
    ) * (1.0 / math.sqrt(HDIM)) + bias
    peak = jnp.max(scores, axis=-1, keepdims=True)
    weights = jnp.exp(scores - peak)
    total = jnp.sum(weights, axis=-1, keepdims=True)
    partial = jnp.dot(weights.astype(jnp.bfloat16), v_ref[0, 0, :, cols], preferred_element_type=jnp.float32)
    return partial, peak, total


def three_parts(value):
    parts = []
    for _ in range(3):
        part = value.astype(jnp.bfloat16).astype(jnp.float32)
        parts.append(part)
        value = value - part
    return parts


def far_kernel(heads, q_ref, k_ref, v_ref, bias_ref, out_ref):
    bias = bias_ref[0]
    lane = lax.broadcasted_iota(jnp.int32, (bias.shape[0], LANES), 1)
    stats = jnp.zeros(lane.shape, jnp.float32)
    for head in range(heads):
        partial, peak, total = one_slot(q_ref, k_ref, v_ref, bias, head)
        out_ref[0, 0, :, pl.ds(head * HDIM, HDIM)] = (partial / total).astype(out_ref.dtype)
        for at, part in enumerate(three_parts(peak) + three_parts(total)):
            stats = jnp.where(lane == at * heads + head, part, stats)
    out_ref[0, 0, :, pl.ds(heads * HDIM, LANES)] = stats.astype(out_ref.dtype)


def read_stats(ref, heads):
    stats = ref[0, 0, :, pl.ds(heads * HDIM, LANES)].astype(jnp.float32)
    parts = [stats[:, at * heads : (at + 1) * heads] for at in range(6)]
    return parts[0] + parts[1] + parts[2], parts[3] + parts[4] + parts[5]


def merge_kernel(heads, near_ref, back_ref, so_far_ref, out_ref):
    near_peak, near_total = read_stats(near_ref, heads)
    far_peak, far_total = read_stats(back_ref, heads)
    top = jnp.maximum(near_peak, far_peak)
    near_w = near_total * jnp.exp(near_peak - top)
    far_w = far_total * jnp.exp(far_peak - top)
    scale = 1.0 / (near_w + far_w)
    near_w, far_w = near_w * scale, far_w * scale
    for head in range(heads):
        cols = pl.ds(head * HDIM, HDIM)
        mixed = near_ref[0, 0, :, cols] * near_w[:, head : head + 1]
        mixed += back_ref[0, 0, :, cols].astype(jnp.float32) * far_w[:, head : head + 1]
        out_ref[0, 0, :, cols] = mixed.astype(jnp.bfloat16)


def near_kernel(heads, q_ref, k_ref, v_ref, bias_ref, back_ref, *rest):
    out_ref = rest[-1]
    bias = bias_ref[0]
    far_peaks, far_totals = read_stats(back_ref, heads)
    for head in range(heads):
        cols = pl.ds(head * HDIM, HDIM)
        partial, peak, total = one_slot(q_ref, k_ref, v_ref, bias, head)
        far_peak, far_total = far_peaks[:, head : head + 1], far_totals[:, head : head + 1]
        top = jnp.maximum(peak, far_peak)
        near_w = jnp.exp(peak - top)
        far_w = jnp.exp(far_peak - top) * far_total
        upper = partial * near_w + back_ref[0, 0, :, cols].astype(jnp.float32) * far_w
        out_ref[0, 0, :, cols] = (upper / (total * near_w + far_w)).astype(jnp.bfloat16)


def plane_spec(array, plane):
    return pl.BlockSpec((1, 1) + array.shape[2:], lambda g: (g, plane, 0, 0))


def attend_cost(groups, rows, keys, width):
    return pl.CostEstimate(
        flops=150 * groups * rows * keys * width, bytes_accessed=8 * groups * rows * width, transcendentals=0
    )


def far_part(operands, bias, kind=jnp.bfloat16):
    groups, rows, keys = bias.shape
    width = operands[0][0].shape[-1]
    return pl.pallas_call(
        functools.partial(far_kernel, width // HDIM),
        grid=(groups,),
        in_specs=[plane_spec(a, p) for a, p in operands] + [pl.BlockSpec((1, rows, keys), lambda g: (g, 0, 0))],
        out_specs=pl.BlockSpec((1, 1, rows, width + LANES), lambda g: (g, 0, 0, 0)),
        out_shape=jax.ShapeDtypeStruct((groups, 1, rows, width + LANES), kind),
        cost_estimate=attend_cost(groups, rows, keys, width),
        name="far_slot",
    )(*[a for a, _ in operands], bias)


def near_part(operands, bias, back, back_plane, plane, planes, so_far):
    groups, rows, keys = bias.shape
    width = operands[0][0].shape[-1]
    in_specs = [plane_spec(a, p) for a, p in operands]
    in_specs += [pl.BlockSpec((1, rows, keys), lambda g: (g, 0, 0)), plane_spec(back, back_plane)]
    args = [a for a, _ in operands] + [bias, back]
    aliases = {}
    if so_far is not None:
        in_specs.append(pl.BlockSpec(memory_space=pl.ANY))
        args.append(so_far)
        aliases = {len(args) - 1: 0}
    return pl.pallas_call(
        functools.partial(near_kernel, width // HDIM),
        grid=(groups,),
        in_specs=in_specs,
        out_specs=pl.BlockSpec((1, 1, rows, width), lambda g: (g, plane, 0, 0)),
        out_shape=jax.ShapeDtypeStruct((groups, planes, rows, width), jnp.bfloat16),
        input_output_aliases=aliases,
        cost_estimate=attend_cost(groups, rows, keys, width),
        name="near_slot",
    )(*args)


def merge_part(near, back, plane, so_far):
    groups, planes, rows, width = so_far.shape
    return pl.pallas_call(
        functools.partial(merge_kernel, width // HDIM),
        grid=(groups,),
        in_specs=[plane_spec(near, 0), plane_spec(back, 0), pl.BlockSpec(memory_space=pl.ANY)],
        out_specs=pl.BlockSpec((1, 1, rows, width), lambda g: (g, plane, 0, 0)),
        out_shape=jax.ShapeDtypeStruct(so_far.shape, so_far.dtype),
        input_output_aliases={2: 0},
        name="merge_slots",
    )(near, back, so_far)


def cut_lines(array, scenes, size):
    groups, planes, positions, width = array.shape
    lines, own = groups // scenes, positions // size
    return array.reshape(scenes, lines, planes, size, own, width).transpose(3, 0, 2, 4, 1, 5)


def swap_cut(cut):
    got = lax.all_to_all(cut, "seq", split_axis=0, concat_axis=0, tiled=True)
    return got, got.transpose(1, 3, 2, 0, 4, 5)


def keep_bias(codes, keys):
    column = jnp.arange(keys)
    kept = jnp.where(column < keys // 2, (codes % 2 == 1)[..., None], (codes >= 2)[..., None])
    return jnp.where(kept, 0.0, -jnp.inf).astype(jnp.float32)


def on_device(size, tokens, queries, key_weight, value_weight, halves):
    scenes, lines, planes, positions, depth = tokens.shape
    width = queries.shape[-1]
    groups = scenes * lines
    q_home = queries.reshape(groups, planes, positions, width)

    def cut(*arrays):
        return jnp.concatenate([cut_lines(a, scenes, size) for a in arrays], axis=2)

    def swap(blocks, *after):
        blocks = lax.optimization_barrier((blocks,) + after)[0]
        got, turned = swap_cut(blocks)
        return got, turned.reshape(-1, turned.shape[2], size * turned.shape[4], turned.shape[5])

    flat_codes = halves.reshape(-1)
    padded = -(-flat_codes.size // (8 * LANES)) * 8 * LANES
    code_tile = jnp.pad(flat_codes, (0, padded - flat_codes.size)).reshape(-1, LANES)
    code_all, key_all, value_all = gather_all(size, code_tile, key_weight, value_weight)
    code_all = code_all.reshape(size, -1)[:, : flat_codes.size].reshape((size,) + halves.shape)
    code_all = jnp.moveaxis(code_all, 0, 1).reshape(scenes, size * lines, planes, 2, 2)

    q0_got, q0 = swap(cut(q_home[:, :1]))
    q12_got, q12 = swap(cut(q_home[:, 1:]), key_all)

    home_rows = tokens.reshape(-1, depth)
    home_shape = (groups, planes, positions, width)
    keys = jnp.dot(home_rows, key_all.reshape(depth, width), preferred_element_type=jnp.float32)
    keys = keys.astype(jnp.bfloat16).reshape(home_shape)
    values = jnp.dot(home_rows, value_all.reshape(depth, width), preferred_element_type=jnp.float32)
    values = values.astype(jnp.bfloat16).reshape(home_shape)

    own = positions // size
    own_half = (lax.axis_index("seq") * own + jnp.arange(own)) // (positions // 2)
    home_half = jnp.arange(positions) // (positions // 2)

    def far_bias(plane):
        pairs = code_all[:, None, :, plane, :, 1]
        codes = jnp.where(own_half[None, :, None] == 0, pairs[..., 0], pairs[..., 1])
        return keep_bias(codes.reshape(scenes * own, size * lines), size * lines)

    def near_bias(plane):
        pairs = halves[:, :, plane, :, 0].reshape(groups, 1, 2)
        codes = jnp.where(home_half[None, :] == 0, pairs[..., 0], pairs[..., 1])
        return keep_bias(codes, positions)

    kv2_got, kv2 = swap(cut(keys[:, 2:], values[:, 2:]), q0_got, q12_got)
    kv1_got, kv1 = swap(cut(keys[:, 1:2], values[:, 1:2]), kv2_got)
    far0 = far_part(((q0, 0), (keys, 2), (values, 2)), far_bias(0))
    far1 = far_part(((q12, 0), (kv2, 0), (kv2, 1)), far_bias(1))
    back01_got, back01 = swap(cut(far0, far1), kv1_got)
    far2 = far_part(((q12, 1), (kv1, 0), (kv1, 1)), far_bias(2))
    kv0_cut, far2_cut = lax.optimization_barrier((cut(keys[:, :1], values[:, :1]), cut(far2)))
    kv0_got, kv0 = swap(kv0_cut, back01_got)
    out = near_part(((q_home, 0), (keys, 1), (values, 1)), near_bias(0), back01, 0, 0, planes, None)
    out = near_part(((q_home, 1), (keys, 0), (values, 0)), near_bias(1), back01, 1, 1, planes, out)
    far2_cut, out = lax.optimization_barrier((far2_cut, out))
    _, back2 = swap(far2_cut, kv0_got)
    near2 = far_part(((q_home, 2), (kv0, 0), (kv0, 1)), near_bias(2), jnp.float32)
    out = merge_part(near2, back2, 2, out)
    return out.reshape(queries.shape)


def solution(mesh):
    lines = P("parts", "seq", None, None, None)
    rows = P("seq", None)
    return jax.shard_map(
        functools.partial(on_device, mesh.shape["seq"]),
        mesh=mesh,
        in_specs=(lines, lines, rows, rows, lines),
        out_specs=lines,
        check_vma=False,
    )
```
